256 devices in a mesh: train: 32 (over y, z), query: 8 (over x, core).
Axes of the slice: x: 4, y: 4, z: 8, core: 2. Of those that a mesh axis runs over, the one named last changes fastest.
Arguments:
- train_grads: float32 [65536, 1024], P(('train', 'query'))
- queries: float32 [2048, 1024], P('query'), may hold values from -6 to 6
Outputs:
- scores: float32 [65536, 2048], P('train', 'query')
The draws below stay inside these ranges and needn't reach their ends.
All inputs are finite; a program needn't handle non-finite values.
Results may differ from the reference program's by a relative error of at most 0.0003.
Values sent between devices are 32-bit elements; how exact they have to be, the bound alone decides.
A program may use at most 128 MiB of HBM per device.

```python
import math
import jax
import jax.numpy as jnp
from jax import lax

K = 1024
TRAIN = 65536
NQ = 2048


def draw_train_grads(key, part):
    key = jax.random.fold_in(key, 11)
    first, second = jax.random.split(key, 2)
    base = jax.random.normal(first, (TRAIN, K), jnp.float32)
    mixed = base + 0.6 * jnp.roll(base, 1, axis=1) + 0.4 * jnp.roll(base, 9, axis=1)
    scale = jnp.exp(jax.random.uniform(second, (TRAIN, 1), jnp.float32, math.log(0.3), math.log(3.0)))
    rise = jnp.exp(0.5 * math.log(3.0) * jnp.arange(TRAIN, dtype=jnp.float32) / TRAIN)[:, None]
    return (mixed * scale * rise).astype(jnp.float32)


def levels(own_key, extent, shards, least, top_value):
    def one(axis_at, parts):
        draws = jax.random.uniform(jax.random.fold_in(jax.random.fold_in(own_key, 6), axis_at), (parts,), jnp.float32, least / len(shards), top_value / len(shards))
        return jnp.repeat(jnp.exp(draws), extent[axis_at] // parts).reshape((-1,) + (1,) * (len(extent) - axis_at - 1))

    level = one(*shards[0])
    for cut in shards[1:]:
        level = level * one(*cut)
    return level


def normal_values(stream_key, dims, deviation, most, cuts=(), kind=jnp.bfloat16):
    drawn = deviation * jax.random.normal(stream_key, dims, jnp.float32)
    if cuts:
        drawn = drawn * levels(stream_key, dims, cuts, -0.22, 0.18)
    return jnp.clip(drawn, -most, most).astype(kind)


def setup_inputs(seed: int = 0) -> dict:
    key_list = jax.random.split(jax.random.key(seed), 3)
    return {
        "train_grads": draw_train_grads(jax.random.fold_in(key_list[2], 71), 0),
        "queries": normal_values(key_list[1], (NQ, K), 1.0, 6.0, ((0, 8),), jnp.float32),
    }


def precondition(fisher, queries):
    width = fisher.shape[0]
    damp = 0.1 * jnp.trace(fisher) / width
    lower = jnp.linalg.cholesky(fisher + damp * jnp.eye(width, dtype=fisher.dtype))
    middle = lax.linalg.triangular_solve(lower, queries.T, left_side=True, lower=True)
    return lax.linalg.triangular_solve(lower, middle, left_side=True, lower=True, transpose_a=True)

def reference(train_grads, queries):
    fisher = jnp.dot(train_grads.T.astype(jnp.float32), train_grads.astype(jnp.float32), precision=lax.Precision.HIGHEST, preferred_element_type=jnp.float32) / TRAIN
    precond = precondition(fisher, queries)
    scores = jnp.dot(train_grads.astype(jnp.float32), precond.astype(jnp.float32), precision=lax.Precision.HIGHEST, preferred_element_type=jnp.float32)
    return scores / jnp.sqrt(jnp.float32(K))
```

```python
import functools
import jax
import jax.numpy as jnp
from jax import lax
from jax.experimental import pallas as pl
from jax.experimental.pallas import tpu as pltpu
from jax.sharding import PartitionSpec as P
B=128; NB=8; K=1024
YB=20; ZB=16
NY,NZ,NX=4,8,4
RY,RZ=YB*B,ZB*B
MESH=pl.DeviceIdType.MESH

def sum_kernel(p_ref, o_ref, w_ref, s1, sy2, sz2, sy3, sz3, sy4, sz4, ssem, rsem):
    t=lax.axis_index("train"); q=lax.axis_index("query")
    y,z=t//NZ, lax.rem(t,NZ)
    x,c=q//2, lax.rem(q,2)
    def at(dx=0,dy=0,dz=0,dc=0):
        return (lax.rem(y+dy,NY)*NZ+lax.rem(z+dz,NZ), lax.rem(x+dx,NX)*2+lax.rem(c+dc,2))
    peers=[at(dc=1)]+[at(dx=d) for d in range(1,NX)]+[at(dy=d) for d in range(1,NY)]+[at(dz=d) for d in range(1,NZ)]
    bar=pltpu.get_barrier_semaphore()
    for dev in peers: pl.semaphore_signal(bar,inc=1,device_id=dev,device_id_type=MESH)
    pl.semaphore_wait(bar,len(peers))
    n=[0]
    def send(src,dst,dev):
        i=n[0]; n[0]+=1
        cp=pltpu.make_async_remote_copy(src_ref=src,dst_ref=dst,send_sem=ssem.at[i],recv_sem=rsem.at[i],device_id=dev,device_id_type=MESH)
        cp.start()
        return cp
    def rows(base,i,size): return pl.ds(pl.multiple_of(base+i*size,8),size)
    pending=[]
    def finish(cps):
        for cp in cps: cp.wait_recv()
        pending.extend(cps)
    hy,hz=RY//2,RZ//2
    a=[send(p_ref.at[rows(0,1-c,hy)],s1.at[pl.ds(0,hy)],at(dc=1)),
       send(p_ref.at[rows(RY,1-c,hz)],s1.at[pl.ds(hy,hz)],at(dc=1))]
    finish(a)
    w_ref[pl.ds(0,hy)]=p_ref[rows(0,c,hy)]+s1[pl.ds(0,hy)]
    w_ref[pl.ds(hy,hz)]=p_ref[rows(RY,c,hz)]+s1[pl.ds(hy,hz)]
    uy,uz=hy//NY,hz//NZ
    a=[send(w_ref.at[rows(0,lax.rem(y+d,NY),uy)],sy2.at[d-1],at(dy=d)) for d in range(1,NY)]
    b=[send(w_ref.at[rows(hy,lax.rem(z+d,NZ),uz)],sz2.at[d-1],at(dz=d)) for d in range(1,NZ)]
    finish(a)
    vy=w_ref[rows(0,y,uy)]
    for d in range(NY-1): vy=vy+sy2[d]
    sy2[NY-1]=vy
    finish(b)
    vz=w_ref[rows(hy,z,uz)]
    for d in range(NZ-1): vz=vz+sz2[d]
    sz2[NZ-1]=vz
    ty,tz=uy//NZ,uz//NY
    a=[send(sy2.at[NY-1,rows(0,lax.rem(z+d,NZ),ty)],sy3.at[d-1],at(dz=d)) for d in range(1,NZ)]
    b=[send(sz2.at[NZ-1,rows(0,lax.rem(y+d,NY),tz)],sz3.at[d-1],at(dy=d)) for d in range(1,NY)]
    finish(a)
    vy=sy2[NY-1,rows(0,z,ty)]
    for d in range(NZ-1): vy=vy+sy3[d]
    sy4[NX-1]=vy
    finish(b)
    vz=sz2[NZ-1,rows(0,y,tz)]
    for d in range(NY-1): vz=vz+sz3[d]
    sz4[NX-1]=vz
    a=[send(sy4.at[NX-1],sy4.at[d-1],at(dx=d)) for d in range(1,NX)]
    b=[send(sz4.at[NX-1],sz4.at[d-1],at(dx=d)) for d in range(1,NX)]
    oy,oz=c*hy,RY+c*hz
    py=oy+y*uy+z*ty
    pz=oz+z*uz+y*tz
    finish(a)
    o_ref[pl.ds(pl.multiple_of(py,8),ty)]=(sy4[0]+sy4[1])+(sy4[2]+sy4[3])
    finish(b)
    o_ref[pl.ds(pl.multiple_of(pz,8),tz)]=(sz4[0]+sz4[1])+(sz4[2]+sz4[3])
    me=o_ref.at[pl.ds(pl.multiple_of(py,8),ty)]
    a=[send(me,me,at(dz=d)) for d in range(1,NZ)]
    me=o_ref.at[pl.ds(pl.multiple_of(pz,8),tz)]
    b=[send(me,me,at(dy=d)) for d in range(1,NY)]
    finish(a)
    me=o_ref.at[rows(oy,y,uy)]
    a=[send(me,me,at(dy=d)) for d in range(1,NY)]
    finish(b)
    me=o_ref.at[rows(oz,z,uz)]
    b=[send(me,me,at(dz=d)) for d in range(1,NZ)]
    finish(a)
    me=o_ref.at[rows(0,c,hy)]
    a=[send(me,me,at(dc=1))]
    finish(b)
    me=o_ref.at[rows(RY,c,hz)]
    b=[send(me,me,at(dc=1))]
    finish(a); finish(b)
    for cp in pending: cp.wait_send()

NSEND=2+(NY-1+NZ-1)*4+2*(NX-1)+2
def sum_blocks(p):
    f32=jnp.float32
    hy,hz=RY//2,RZ//2
    uy,uz=hy//NY,hz//NZ
    ty,tz=uy//NZ,uz//NY
    return pl.pallas_call(sum_kernel,out_shape=jax.ShapeDtypeStruct(p.shape,f32),
      in_specs=[pl.BlockSpec(memory_space=pltpu.VMEM)],out_specs=pl.BlockSpec(memory_space=pltpu.VMEM),
      scratch_shapes=[pltpu.VMEM((hy+hz,B),f32),pltpu.VMEM((hy+hz,B),f32),
        pltpu.VMEM((NY,uy,B),f32),pltpu.VMEM((NZ,uz,B),f32),
        pltpu.VMEM((NZ-1,ty,B),f32),pltpu.VMEM((NY-1,tz,B),f32),
        pltpu.VMEM((NX,ty,B),f32),pltpu.VMEM((NX,tz,B),f32),
        pltpu.SemaphoreType.DMA((NSEND,)),pltpu.SemaphoreType.DMA((NSEND,))],
      compiler_params=pltpu.CompilerParams(collective_id=0,has_side_effects=True,vmem_limit_bytes=32*2**20))(p)


HI=lax.Precision.HIGHEST
def dotp(a,b,dims,prec=HI):
    return lax.dot_general(a,b,(dims,((),())),precision=prec,preferred_element_type=jnp.float32)
def rcp(d):
    r=pltpu.reciprocal(d,approx=True)
    return r*(2.0-d*r)
def leaf(a, G=16):
    nv=G//8
    rows=[a[8*i:8*i+8,:] for i in range(16)]
    lane=lax.broadcasted_iota(jnp.int32,(8,128),1)
    sub=lax.broadcasted_iota(jnp.int32,(8,128),0)
    bl=lambda x,c: jnp.broadcast_to(x[:,c:c+1],(8,128))
    bs=lambda x,s: jnp.broadcast_to(x[s:s+1,:],(8,128))
    for g in range(128//G):
        R=[rows[nv*g+v] for v in range(nv)]
        C=[[bl(R[v],G*g+c) for v in range(nv)] for c in range(G)]
        inb=(lane>=G*g)&(lane<G*g+G)
        RA=[jnp.where(inb, jnp.where(lane-G*g-8*v==sub,1.0,0.0), R[v]) for v in range(nv)]
        for j in range(G):
            jv,js=divmod(j,8)
            r=rcp(bs(C[j][jv],js))
            cr=[jnp.where(sub==js,1.0-r,C[j][v]*r) if v==jv else C[j][v]*r for v in range(nv)]
            for c in range(j+1,G):
                rj=bs(C[c][jv],js)
                for v in range(nv): C[c][v]=C[c][v]-cr[v]*rj
            rr=bs(RA[jv],js)
            for v in range(nv): RA[v]=RA[v]-cr[v]*rr
        rb=[bs(RA[c//8],c%8) for c in range(G)]
        new=list(rows)
        for v in range(nv): new[nv*g+v]=RA[v]
        for i in range(16):
            if i//nv==g: continue
            cols=[bl(rows[i],G*g+c) for c in range(G)]
            p=[cols[c]*rb[c] for c in range(G)]
            while len(p)>1: p=[p[2*k]+p[2*k+1] for k in range(len(p)//2)]
            new[i]=jnp.where(inb,0.0,rows[i])-p[0]
        rows=new
    return jnp.concatenate(rows,0)

def bidx(i,j): return i*NB-i*(i-1)//2+(j-i)

def factor_kernel(total,p_ref,q_ref,o_ref,m_ref,b_ref,y_ref):
    eye=(lax.broadcasted_iota(jnp.int32,(B,B),0)==lax.broadcasted_iota(jnp.int32,(B,B),1))
    dg=jnp.zeros((B,B),jnp.float32)
    for i in range(NB): dg=dg+jnp.where(eye,p_ref[bidx(i,i)]*(1.0/total),0.0)
    trace=jnp.sum(jnp.sum(dg,axis=0,keepdims=True),axis=1,keepdims=True)
    damp=0.1*trace/K
    inv=1.0/damp
    scale=jnp.broadcast_to(inv*(1.0/total),(1,B))
    for i in range(NB):
        for j in range(i,NB):
            v=p_ref[bidx(i,j)]*scale
            if i==j: v=jnp.where(eye,v+1.0,v)
            m_ref[i,:,j*B:(j+1)*B]=v
    b_ref[...]=q_ref[...]
    for k in range(NB):
        s=k*B; e=s+B
        dinv=leaf(m_ref[k,:,s:e])
        z=dotp(b_ref[:,s:e],dinv,((1,),(0,)))
        if k<NB-1:
            a=m_ref[k,:,e:]
            y=dotp(dinv,a,((1,),(0,)))
            y_ref[k,:,e:]=y
            for i in range(k+1,NB):
                m_ref[i,:,i*B:]-=dotp(a[:,(i-k-1)*B:(i-k)*B],y[:,(i-k-1)*B:],((0,),(0,)))
            b_ref[:,e:]-=dotp(z,a,((1,),(0,)))
        b_ref[:,s:e]=z
    for k in range(NB-2,-1,-1):
        s=k*B; e=s+B
        b_ref[:,s:e]-=dotp(b_ref[:,e:],y_ref[k,:,e:],((1,),(1,)))
    o_ref[...]=b_ref[...]*jnp.broadcast_to(inv*(1.0/jnp.sqrt(jnp.float32(K))),(1,K))

def factor(p,q,total):
    nq=q.shape[0]
    return pl.pallas_call(functools.partial(factor_kernel,total),
        out_shape=jax.ShapeDtypeStruct((nq,K),jnp.float32),
        scratch_shapes=[pltpu.VMEM((NB,B,K),jnp.float32),pltpu.VMEM((nq,K),jnp.float32),pltpu.VMEM((NB,B,K),jnp.float32)],
        compiler_params=pltpu.CompilerParams(vmem_limit_bytes=40*2**20))(p,q)


def gram_kernel(x_ref, p_ref):
    for i in range(NB):
        rows = dotp(x_ref[:, i * B:(i + 1) * B], x_ref[:, i * B:], ((0,), (0,)))
        for j in range(i, NB):
            at = bidx(i, j) * B
            p_ref[at:at + B, :] = rows[:, (j - i) * B:(j - i + 1) * B]


def gram(x):
    return pl.pallas_call(
        gram_kernel,
        out_shape=jax.ShapeDtypeStruct((NB * (NB + 1) // 2 * B, B), jnp.float32),
        compiler_params=pltpu.CompilerParams(vmem_limit_bytes=32 * 2**20),
    )(x)


def local(train_grads, queries):
    total = train_grads.shape[0] * lax.axis_size("train") * lax.axis_size("query")
    summed = sum_blocks(gram(train_grads))
    precond = factor(summed.reshape(-1, B, B), queries, float(total))
    rows = lax.all_gather(train_grads, "query", axis=0, tiled=True)
    return lax.dot_general(
        rows,
        precond,
        (((1,), (1,)), ((), ())),
        precision=lax.Precision.HIGH,
        preferred_element_type=jnp.float32,
    )


def solution(mesh):
    in_specs = (P(("train", "query"), None), P("query", None))
    out_specs = P("train", "query")
    return jax.shard_map(local, mesh=mesh, in_specs=in_specs, out_specs=out_specs, check_vma=False)
```

```python
import functools
import jax
import jax.numpy as jnp
from jax import lax
from jax.experimental import pallas as pl
from jax.experimental.pallas import tpu as pltpu
from jax.sharding import PartitionSpec as P

f32 = jnp.float32
bf = jnp.bfloat16
B=128; NB=8; K=1024
YB=20; ZB=16
NY,NZ,NX=4,8,4
RY,RZ=YB*B,ZB*B
MESH=pl.DeviceIdType.MESH

def sum_kernel(p_ref, o_ref, w_ref, s1, sy2, sz2, sy3, sz3, sy4, sz4, ssem, rsem):
    t=lax.axis_index("train"); q=lax.axis_index("query")
    y,z=t//NZ, lax.rem(t,NZ)
    x,c=q//2, lax.rem(q,2)
    def at(dx=0,dy=0,dz=0,dc=0):
        return (lax.rem(y+dy,NY)*NZ+lax.rem(z+dz,NZ), lax.rem(x+dx,NX)*2+lax.rem(c+dc,2))
    peers=[at(dc=1)]+[at(dx=d) for d in range(1,NX)]+[at(dy=d) for d in range(1,NY)]+[at(dz=d) for d in range(1,NZ)]
    bar=pltpu.get_barrier_semaphore()
    for dev in peers: pl.semaphore_signal(bar,inc=1,device_id=dev,device_id_type=MESH)
    pl.semaphore_wait(bar,len(peers))
    n=[0]
    def send(src,dst,dev):
        i=n[0]; n[0]+=1
        cp=pltpu.make_async_remote_copy(src_ref=src,dst_ref=dst,send_sem=ssem.at[i],recv_sem=rsem.at[i],device_id=dev,device_id_type=MESH)
        cp.start()
        return cp
    def rows(base,i,size): return pl.ds(pl.multiple_of(base+i*size,8),size)
    pending=[]
    def finish(cps):
        for cp in cps: cp.wait_recv()
        pending.extend(cps)
    hy,hz=RY//2,RZ//2
    a=[send(p_ref.at[rows(0,1-c,hy)],s1.at[pl.ds(0,hy)],at(dc=1)),
       send(p_ref.at[rows(RY,1-c,hz)],s1.at[pl.ds(hy,hz)],at(dc=1))]
    finish(a)
    w_ref[pl.ds(0,hy)]=p_ref[rows(0,c,hy)]+s1[pl.ds(0,hy)]
    w_ref[pl.ds(hy,hz)]=p_ref[rows(RY,c,hz)]+s1[pl.ds(hy,hz)]
    uy,uz=hy//NY,hz//NZ
    a=[send(w_ref.at[rows(0,lax.rem(y+d,NY),uy)],sy2.at[d-1],at(dy=d)) for d in range(1,NY)]
    b=[send(w_ref.at[rows(hy,lax.rem(z+d,NZ),uz)],sz2.at[d-1],at(dz=d)) for d in range(1,NZ)]
    finish(a)
    vy=w_ref[rows(0,y,uy)]
    for d in range(NY-1): vy=vy+sy2[d]
    sy2[NY-1]=vy
    finish(b)
    vz=w_ref[rows(hy,z,uz)]
    for d in range(NZ-1): vz=vz+sz2[d]
    sz2[NZ-1]=vz
    ty,tz=uy//NZ,uz//NY
    a=[send(sy2.at[NY-1,rows(0,lax.rem(z+d,NZ),ty)],sy3.at[d-1],at(dz=d)) for d in range(1,NZ)]
    b=[send(sz2.at[NZ-1,rows(0,lax.rem(y+d,NY),tz)],sz3.at[d-1],at(dy=d)) for d in range(1,NY)]
    finish(a)
    vy=sy2[NY-1,rows(0,z,ty)]
    for d in range(NZ-1): vy=vy+sy3[d]
    sy4[NX-1]=vy
    finish(b)
    vz=sz2[NZ-1,rows(0,y,tz)]
    for d in range(NY-1): vz=vz+sz3[d]
    sz4[NX-1]=vz
    a=[send(sy4.at[NX-1],sy4.at[d-1],at(dx=d)) for d in range(1,NX)]
    b=[send(sz4.at[NX-1],sz4.at[d-1],at(dx=d)) for d in range(1,NX)]
    oy,oz=c*hy,RY+c*hz
    py=oy+y*uy+z*ty
    pz=oz+z*uz+y*tz
    finish(a)
    o_ref[pl.ds(pl.multiple_of(py,8),ty)]=(sy4[0]+sy4[1])+(sy4[2]+sy4[3])
    finish(b)
    o_ref[pl.ds(pl.multiple_of(pz,8),tz)]=(sz4[0]+sz4[1])+(sz4[2]+sz4[3])
    me=o_ref.at[pl.ds(pl.multiple_of(py,8),ty)]
    a=[send(me,me,at(dz=d)) for d in range(1,NZ)]
    me=o_ref.at[pl.ds(pl.multiple_of(pz,8),tz)]
    b=[send(me,me,at(dy=d)) for d in range(1,NY)]
    finish(a)
    me=o_ref.at[rows(oy,y,uy)]
    a=[send(me,me,at(dy=d)) for d in range(1,NY)]
    finish(b)
    me=o_ref.at[rows(oz,z,uz)]
    b=[send(me,me,at(dz=d)) for d in range(1,NZ)]
    finish(a)
    me=o_ref.at[rows(0,c,hy)]
    a=[send(me,me,at(dc=1))]
    finish(b)
    me=o_ref.at[rows(RY,c,hz)]
    b=[send(me,me,at(dc=1))]
    finish(a); finish(b)
    for cp in pending: cp.wait_send()

NSEND=2+(NY-1+NZ-1)*4+2*(NX-1)+2

def leaf(a, G=16):
    nv=G//8; ng=B//G
    lane=lax.broadcasted_iota(jnp.int32,(8,B),1)
    sub=lax.broadcasted_iota(jnp.int32,(8,B),0)
    bl=lambda x,c: jnp.broadcast_to(x[:,c:c+1],(8,B))
    bs=lambda x,s: jnp.broadcast_to(x[s:s+1,:],(8,B))
    rows=[a[8*i:8*i+8,:] for i in range(16)]
    for g in range(ng):
        R=[rows[nv*g+v] for v in range(nv)]
        C=[[bl(R[v],G*g+c) for v in range(nv)] for c in range(G)]
        inb=(lane>=G*g)&(lane<G*g+G)
        RA=[jnp.where(inb, jnp.where(lane-G*g-8*v==sub,1.0,0.0), R[v]) for v in range(nv)]
        for j in range(0,G,2):
            jv,js=divmod(j,8)
            a0=bs(C[j][jv],js); b0=bs(C[j+1][jv],js); c0=bs(C[j+1][jv],js+1)
            r=pltpu.reciprocal(a0*c0-b0*b0,approx=True)
            u=[];w=[]
            for v in range(nv):
                cj,ck=C[j][v],C[j+1][v]
                if v==jv:
                    cj=jnp.where(sub==js,cj-1.0,cj); ck=jnp.where(sub==js+1,ck-1.0,ck)
                u.append(cj*c0-ck*b0); w.append(ck*a0-cj*b0)
            for c in range(j+2,G):
                x0=bs(C[c][jv],js); x1=bs(C[c][jv],js+1)
                for v in range(nv): C[c][v]=C[c][v]-(u[v]*x0+w[v]*x1)*r
            x0=bs(RA[jv],js); x1=bs(RA[jv],js+1)
            for v in range(nv): RA[v]=RA[v]-(u[v]*x0+w[v]*x1)*r
        new=list(rows)
        for v in range(nv): new[nv*g+v]=RA[v]
        near=[i for i in range(16) if i//nv==g+1]
        rb=[bs(RA[c//8],c%8) for c in range(G)] if near else []
        for i in near:
            p=[bl(rows[i],G*g+c)*rb[c] for c in range(G)]
            while len(p)>1: p=[p[2*k]+p[2*k+1] for k in range(len(p)//2)]
            new[i]=jnp.where(inb,0.0,rows[i])-p[0]
        rest=[i for i in range(16) if i//nv!=g and i not in near]
        zero=jnp.zeros((8,B),f32)
        d=lax.dot_general(jnp.concatenate([rows[i] for i in rest],0),
            jnp.concatenate([RA[i-nv*g] if i//nv==g else zero for i in range(16)],0),
            (((1,),(0,)),((),())),precision=lax.Precision.HIGHEST,preferred_element_type=f32)
        for m,i in enumerate(rest): new[i]=jnp.where(inb,0.0,rows[i])-d[8*m:8*m+8]
        rows=new
    return jnp.concatenate(rows,0)

def split(x, n=3):
    out=[]
    for i in range(n):
        h=x.astype(bf); out.append(h)
        if i<n-1: x=x-h.astype(f32)
    return out
TERMS={6:[(0,0),(0,1),(1,0),(0,2),(2,0),(1,1)],3:[(0,0),(0,1),(1,0)],4:[(0,0),(0,1),(1,0),(1,1)]}
def dots(a,b,nt,n=6):
    t=TERMS[n]
    l=jnp.concatenate([a[i] for i,_ in t],axis=1)
    r=jnp.concatenate([b[j] for _,j in t],axis=1 if nt else 0)
    return lax.dot_general(l,r,(((1,),(1,) if nt else (0,)),((),())),preferred_element_type=f32)
def part(s,sl): return [x[sl] for x in s]
OFF=[sum((NB-i)*B for i in range(k)) for k in range(NB+1)]
def factor_kernel(total,order,n,p_ref,q_ref,o_ref,m_ref,b_ref,*y_refs):
    ns=3 if n==6 else 2
    sp=lambda x: split(x,ns)
    eye=(lax.broadcasted_iota(jnp.int32,(B,B),0)==lax.broadcasted_iota(jnp.int32,(B,B),1))
    dg=jnp.zeros((B,B),f32)
    for i in range(NB): dg=dg+jnp.where(eye,p_ref[OFF[i]:OFF[i]+B]*(1.0/total),0.0)
    trace=jnp.sum(jnp.sum(dg,axis=0,keepdims=True),axis=1,keepdims=True)
    damp=0.1*trace/K
    inv=1.0/damp
    scale=jnp.broadcast_to(inv*(1.0/total),(1,B))
    for k in range(NB):
        d=p_ref[OFF[k]:OFF[k]+B]*scale
        m_ref[OFF[k]:OFF[k]+B]=jnp.where(eye,d+1.0,d)
        if k<NB-1: m_ref[OFF[k]+B:OFF[k+1]]=p_ref[OFF[k]+B:OFF[k+1]]*scale
    b_ref[...]=q_ref[...]
    dinv=leaf(m_ref[:B])
    for k in range(NB):
        s=k*B; e=s+B
        ds=sp(dinv)
        if k<NB-1:
            a=sp(m_ref[OFF[k]+B:OFF[k+1]])
            y1=sp(dots(part(a,slice(0,B)),ds,False,n))
            D=m_ref[OFF[k+1]:OFF[k+1]+B]-dots(y1,part(a,slice(0,B)),True,n)
            def rest(ds=ds,a=a,y1=y1,k=k,s=s,e=e):
                rows=(NB-1-k)*B
                y=y1
                if k<NB-2:
                    y2=sp(dots(part(a,slice(B,rows)),ds,False,n))
                    y=[jnp.concatenate([u,v],axis=0) for u,v in zip(y1,y2)]
                    m_ref[OFF[k+1]+B:OFF[k+2]]-=dots(y2,part(a,slice(0,B)),True,n)
                    j=k+2
                    while j<NB:
                        w=2 if j+1<NB else 1
                        o=(j-k-1)*B
                        u=dots(part(y,slice(o,rows)),part(a,slice(o,o+w*B)),True,n)
                        m_ref[OFF[j]:OFF[j+1]]-=u[:,:B]
                        if w==2: m_ref[OFF[j+1]:OFF[j+2]]-=u[B:,B:]
                        j+=w
                for r,v in zip(y_refs,y): r[OFF[k]+B:OFF[k+1]]=v
                z=dots(sp(b_ref[:,s:e]),ds,False,n)
                b_ref[:,e:]-=dots(sp(z),a,True,n)
                b_ref[:,s:e]=z
            if order==0:
                rest(); dinv=leaf(D)
            else:
                dinv=leaf(D); rest()
        else:
            b_ref[:,s:e]=dots(sp(b_ref[:,s:e]),ds,False,n)
    for j in range(NB-1,0,-1):
        x=sp(b_ref[:,j*B:(j+1)*B])
        y=[jnp.concatenate([r[OFF[k]+(j-k)*B:OFF[k]+(j-k+1)*B] for k in range(j)],axis=1) for r in y_refs]
        b_ref[:,:j*B]-=dots(x,y,False,n)
    o_ref[...]=b_ref[...]*jnp.broadcast_to(inv*(1.0/jnp.sqrt(f32(K))),(1,K))

def gram_kernel(x_ref, p_ref):
    for k in range(NB):
        p_ref[OFF[k]:OFF[k + 1], :] = lax.dot_general(
            x_ref[:, k * B:], x_ref[:, k * B:(k + 1) * B], (((0,), (0,)), ((), ())),
            precision=lax.Precision.HIGHEST, preferred_element_type=f32)


def gram(x):
    return pl.pallas_call(
        gram_kernel,
        out_shape=jax.ShapeDtypeStruct((OFF[NB], B), f32),
        compiler_params=pltpu.CompilerParams(vmem_limit_bytes=32 * 2**20),
    )(x)


NCOMM = 10


def solve_kernel(total, p_ref, q_ref, o_ref, sum_ref, *refs):
    sum_kernel(p_ref, sum_ref, *refs[:NCOMM])
    factor_kernel(total, 0, 6, sum_ref, q_ref, o_ref, *refs[NCOMM:])


def solve(p, q, total):
    nq = q.shape[0]
    hy, hz = RY // 2, RZ // 2
    uy, uz = hy // NY, hz // NZ
    ty, tz = uy // NZ, uz // NY
    return pl.pallas_call(
        functools.partial(solve_kernel, total),
        out_shape=jax.ShapeDtypeStruct((nq, K), f32),
        in_specs=[pl.BlockSpec(memory_space=pltpu.VMEM)] * 2,
        out_specs=pl.BlockSpec(memory_space=pltpu.VMEM),
        scratch_shapes=[
            pltpu.VMEM((OFF[NB], B), f32),
            pltpu.VMEM((hy + hz, B), f32), pltpu.VMEM((hy + hz, B), f32),
            pltpu.VMEM((NY, uy, B), f32), pltpu.VMEM((NZ, uz, B), f32),
            pltpu.VMEM((NZ - 1, ty, B), f32), pltpu.VMEM((NY - 1, tz, B), f32),
            pltpu.VMEM((NX, ty, B), f32), pltpu.VMEM((NX, tz, B), f32),
            pltpu.SemaphoreType.DMA((NSEND,)), pltpu.SemaphoreType.DMA((NSEND,)),
            pltpu.VMEM((OFF[NB], B), f32), pltpu.VMEM((nq, K), f32)] + [pltpu.VMEM((OFF[NB], B), bf)] * 3,
        compiler_params=pltpu.CompilerParams(
            collective_id=0, has_side_effects=True, vmem_limit_bytes=40 * 2**20),
    )(p, q)


def local(train_grads, queries):
    total = train_grads.shape[0] * lax.axis_size("train") * lax.axis_size("query")
    precond = solve(gram(train_grads), queries, float(total))
    rows = lax.all_gather(train_grads, "query", axis=0, tiled=True)
    return lax.dot_general(
        rows, precond, (((1,), (1,)), ((), ())),
        precision=lax.Precision.HIGH, preferred_element_type=jnp.float32)


def solution(mesh):
    in_specs = (P(("train", "query"), None), P("query", None))
    out_specs = P("train", "query")
    return jax.shard_map(local, mesh=mesh, in_specs=in_specs, out_specs=out_specs, check_vma=False)
```

```python
import functools
import jax
import jax.numpy as jnp
from jax import lax
from jax.experimental import pallas as pl
from jax.experimental.pallas import tpu as pltpu
from jax.sharding import PartitionSpec as P

f32 = jnp.float32
bf = jnp.bfloat16
B = 128
NB = 8
K = B * NB
NY, NZ, NX = 4, 8, 4
MESH = pl.DeviceIdType.MESH
OFF = [sum((NB - i) * B for i in range(k)) for k in range(NB + 1)]
CHUNKS = [(0, 1024), (1024, 1024), (2048, 1024), (3072, 1024), (4096, 512)]
STAGES = 8
NCOPY = 25 * len(CHUNKS) + 12


def split(x, n=3):
    out = []
    for i in range(n):
        h = x.astype(bf)
        out.append(h)
        if i < n - 1:
            x = x - h.astype(f32)
    return out


TERMS = [(0, 0), (0, 1), (1, 0), (0, 2), (2, 0), (1, 1)]


def dots(a, b, nt):
    l = jnp.concatenate([a[i] for i, _ in TERMS], axis=1)
    r = jnp.concatenate([b[j] for _, j in TERMS], axis=1 if nt else 0)
    dims = (((1,), (1,) if nt else (0,)), ((), ()))
    return lax.dot_general(l, r, dims, preferred_element_type=f32)


def part(s, sl):
    return [x[sl] for x in s]


def leaf(a, G=16):
    nv=G//8; ng=B//G
    lane=lax.broadcasted_iota(jnp.int32,(8,B),1)
    sub=lax.broadcasted_iota(jnp.int32,(8,B),0)
    bl=lambda x,c: jnp.broadcast_to(x[:,c:c+1],(8,B))
    bs=lambda x,s: jnp.broadcast_to(x[s:s+1,:],(8,B))
    rows=[a[8*i:8*i+8,:] for i in range(16)]
    for g in range(ng):
        R=[rows[nv*g+v] for v in range(nv)]
        C=[[bl(R[v],G*g+c) for v in range(nv)] for c in range(G)]
        inb=(lane>=G*g)&(lane<G*g+G)
        RA=[jnp.where(inb, jnp.where(lane-G*g-8*v==sub,1.0,0.0), R[v]) for v in range(nv)]
        for j in range(0,G,2):
            jv,js=divmod(j,8)
            a0=bs(C[j][jv],js); b0=bs(C[j+1][jv],js); c0=bs(C[j+1][jv],js+1)
            r=pltpu.reciprocal(a0*c0-b0*b0,approx=True)
            u=[];w=[]
            for v in range(nv):
                cj,ck=C[j][v],C[j+1][v]
                if v==jv:
                    cj=jnp.where(sub==js,cj-1.0,cj); ck=jnp.where(sub==js+1,ck-1.0,ck)
                u.append(cj*c0-ck*b0); w.append(ck*a0-cj*b0)
            for c in range(j+2,G):
                x0=bs(C[c][jv],js); x1=bs(C[c][jv],js+1)
                for v in range(nv): C[c][v]=C[c][v]-(u[v]*x0+w[v]*x1)*r
            x0=bs(RA[jv],js); x1=bs(RA[jv],js+1)
            for v in range(nv): RA[v]=RA[v]-(u[v]*x0+w[v]*x1)*r
        new=list(rows)
        for v in range(nv): new[nv*g+v]=RA[v]
        near=[i for i in range(16) if i//nv==g+1]
        rb=[bs(RA[c//8],c%8) for c in range(G)] if near else []
        for i in near:
            p=[bl(rows[i],G*g+c)*rb[c] for c in range(G)]
            while len(p)>1: p=[p[2*k]+p[2*k+1] for k in range(len(p)//2)]
            new[i]=jnp.where(inb,0.0,rows[i])-p[0]
        rest=[i for i in range(16) if i//nv!=g and i not in near]
        zero=jnp.zeros((8,B),f32)
        d=lax.dot_general(jnp.concatenate([rows[i] for i in rest],0),
            jnp.concatenate([RA[i-nv*g] if i//nv==g else zero for i in range(16)],0),
            (((1,),(0,)),((),())),precision=lax.Precision.HIGHEST,preferred_element_type=f32)
        for m,i in enumerate(rest): new[i]=jnp.where(inb,0.0,rows[i])-d[8*m:8*m+8]
        rows=new
    return jnp.concatenate(rows,0)


class Links:
    def __init__(self, ssem, rsem):
        t, q = lax.axis_index("train"), lax.axis_index("query")
        self.y, self.z = t // NZ, lax.rem(t, NZ)
        self.x, self.c = q // 2, lax.rem(q, 2)
        self.ssem, self.rsem = ssem, rsem
        self.count = 0
        self.started = []

    def at(self, dx=0, dy=0, dz=0, dc=0):
        return (
            lax.rem(self.y + dy, NY) * NZ + lax.rem(self.z + dz, NZ),
            lax.rem(self.x + dx, NX) * 2 + lax.rem(self.c + dc, 2),
        )

    def send(self, src, dst, device):
        i = self.count
        self.count += 1
        copy = pltpu.make_async_remote_copy(
            src_ref=src, dst_ref=dst, send_sem=self.ssem.at[i], recv_sem=self.rsem.at[i],
            device_id=device, device_id_type=MESH)
        copy.start()
        self.started.append(copy)
        return copy


def arrive(copies):
    for copy in copies:
        copy.wait_recv()


def rows(base, i, size):
    return pl.ds(pl.multiple_of(base + i * size, 8), size)


def total_of(k, chunk, p_ref, o_ref, s1, w, sy, sz, sx):
    base, n = chunk
    h = n // 2
    u = h // NY
    t = u // NZ
    x, y, z, c = k.x, k.y, k.z, k.c
    a = [k.send(p_ref.at[rows(base, 1 - c, h)], s1, k.at(dc=1))]
    yield
    arrive(a)
    w[...] = p_ref[rows(base, c, h)] + s1[...]
    a = [k.send(w.at[rows(0, lax.rem(y + d, NY), u)], sy.at[d - 1], k.at(dy=d)) for d in (2, 1, 3)]
    yield
    arrive(a)
    sy[NY - 1] = (w[rows(0, y, u)] + sy[0]) + (sy[1] + sy[2])
    a = [k.send(sy.at[NY - 1, rows(0, lax.rem(z + d, NZ), t)], sz.at[d - 1], k.at(dz=d))
         for d in (4, 3, 5, 2, 6, 1, 7)]
    yield
    arrive(a)
    v = sy[NY - 1, rows(0, z, t)]
    for d in range(NZ - 1):
        v = v + sz[d]
    sx[NX - 1] = v
    a = [k.send(sx.at[NX - 1], sx.at[d - 1], k.at(dx=d)) for d in (2, 1, 3)]
    yield
    arrive(a)
    own = pl.ds(pl.multiple_of(base + c * h + y * u + z * t, 8), t)
    o_ref[own] = (sx[0] + sx[1]) + (sx[2] + sx[3])
    a = [k.send(o_ref.at[own], o_ref.at[own], k.at(dz=d)) for d in (4, 3, 5, 2, 6, 1, 7)]
    yield
    arrive(a)
    own = rows(base + c * h, y, u)
    a = [k.send(o_ref.at[own], o_ref.at[own], k.at(dy=d)) for d in (2, 1, 3)]
    yield
    arrive(a)
    own = rows(base, c, h)
    a = [k.send(o_ref.at[own], o_ref.at[own], k.at(dc=1))]
    yield
    arrive(a)
    yield


def chunk_scratch(chunk):
    h = chunk[1] // 2
    u = h // NY
    t = u // NZ
    shapes = [(h, B), (h, B), (NY, u, B), (NZ - 1, t, B), (NX, t, B)]
    return [pltpu.VMEM(s, f32) for s in shapes]


def gathered(k, x_ref, g_ref, own_sem):
    n = x_ref.shape[0]
    half = n // 2
    mine = (k.x * 2 + k.c) * n
    below, above = (lax.rem(k.x + NX - 1, NX) * 2 + k.c) * n, (lax.rem(k.x + 1, NX) * 2 + k.c) * n
    across = (lax.rem(k.x + 2, NX) * 2 + k.c) * n
    at = lambda base, first, size: g_ref.at[pl.ds(pl.multiple_of(base + first, 8), size)]
    own = pltpu.make_async_copy(x_ref, at(mine, 0, n), own_sem)
    own.start()
    src = [x_ref.at[pl.ds(i * half, half)] for i in range(2)]
    up = [k.send(src[0], at(mine, 0, half), k.at(dx=1))]
    down = [k.send(src[1], at(mine, half, half), k.at(dx=NX - 1))]
    yield
    up.append(k.send(src[1], at(mine, half, half), k.at(dx=1)))
    down.append(k.send(src[0], at(mine, 0, half), k.at(dx=NX - 1)))
    core = [k.send(x_ref, at(mine, 0, n), k.at(dc=1))]
    arrive([up[0], down[0]])
    lo, hi = at(below, 0, half), at(above, half, half)
    far = [k.send(lo, lo, k.at(dx=1)), k.send(hi, hi, k.at(dx=NX - 1))]
    yield
    arrive([up[1], down[1]])
    for base in (below, above):
        block = at(base, 0, n)
        core.append(k.send(block, block, k.at(dc=1)))
    yield
    arrive(far)
    block = at(across, 0, n)
    core.append(k.send(block, block, k.at(dc=1)))
    yield
    own.wait()
    arrive(core)
    yield


def kernel(total, x_hbm, q_hbm, o_ref, g_ref, x_ref, p_ref, f_ref, m_ref, b_ref, y0_ref, y1_ref, y2_ref,
           ssem, rsem, lsem, *scratch):
    y_refs = (y0_ref, y1_ref, y2_ref)
    k = Links(ssem, rsem)
    load = pltpu.make_async_copy(x_hbm, x_ref, lsem.at[0])
    load.start()
    q_load = pltpu.make_async_copy(q_hbm, b_ref, lsem.at[2])
    q_load.start()
    peers = [k.at(dc=1)] + [k.at(dx=d) for d in range(1, NX)]
    peers += [k.at(dy=d) for d in range(1, NY)] + [k.at(dz=d) for d in range(1, NZ)]
    barrier = pltpu.get_barrier_semaphore()
    for device in peers:
        pl.semaphore_signal(barrier, inc=1, device_id=device, device_id_type=MESH)
    load.wait()

    def gram(j):
        p_ref[OFF[j]:OFF[j + 1]] = lax.dot_general(
            x_ref[:, j * B:], x_ref[:, j * B:(j + 1) * B], (((0,), (0,)), ((), ())),
            precision=lax.Precision.HIGHEST, preferred_element_type=f32)

    row_at = lax.broadcasted_iota(jnp.int32, (B, B), 0)
    column_at = lax.broadcasted_iota(jnp.int32, (B, B), 1)
    corner = (row_at == 0) & (column_at == B - 1)
    eye = row_at == column_at
    squares = jnp.sum(x_ref[...] * x_ref[...], axis=0, keepdims=True) * (1.0 / total)
    gram(0)
    p_ref[:B] = jnp.where(corner, jnp.sum(squares, axis=1, keepdims=True), p_ref[:B])
    pl.semaphore_wait(barrier, len(peers))
    sums = [total_of(k, c, p_ref, f_ref, *scratch[5 * i:5 * i + 5]) for i, c in enumerate(CHUNKS)]
    gather = gathered(k, x_hbm, g_ref, lsem.at[1])
    done = [0] * len(sums)

    def go(*chunks):
        for i in chunks:
            next(sums[i])
            done[i] += 1

    go(0)
    next(gather)
    gram(1)
    gram(2)
    go(1, 0)
    for j in range(3, NB):
        gram(j)
    go(2, 3, 4, 1, 2, 3, 4)
    go(0, 1, 0, 2, 0, 1, 3, 4, 1, 2, 0, 2, 3, 4)
    next(gather)
    go(1, 3, 4, 0, 2, 0)
    d = f_ref[:B]
    trace = d[0:1, B - 1:B]
    damp = 0.1 * trace / K
    inv = 1.0 / damp
    scale = jnp.broadcast_to(inv * (1.0 / total), (1, B))
    d = jnp.where(corner, d[B - 1:B, 0:1], d) * scale
    dinv = leaf(jnp.where(eye, d + 1.0, d))
    q_load.wait()
    due = {0: (1, 3, 4, 1), 1: (2, 2), 2: (3, 4, 3, 4), 4: (-1,), 6: (-1,)}
    for i in range(NB):
        s, e = i * B, i * B + B
        left = (NB - 1 - i) * B
        ds = split(dinv)
        if i == NB - 1:
            b_ref[:, s:e] = dots(split(b_ref[:, s:e]), ds, False)
            break
        for j in due.get(i, ()):
            if j < 0:
                next(gather)
            else:
                go(j)
        first = i == 0
        a = f_ref[OFF[i] + B:OFF[i + 1]] * scale
        if not first:
            a = a + m_ref[OFF[i] + B:OFF[i + 1]]
        a = split(a)
        a1 = part(a, slice(0, B))
        y = split(dots(a1, ds, False))
        d = f_ref[OFF[i + 1]:OFF[i + 1] + B] * scale - dots(y, a1, True)
        d = jnp.where(eye, d + 1.0, d)
        if not first:
            d = d + m_ref[OFF[i + 1]:OFF[i + 1] + B]
        if i < NB - 2:
            y2 = split(dots(part(a, slice(B, left)), ds, False))

            def update(lo, hi, v):
                m_ref[lo:hi] = -v if first else m_ref[lo:hi] - v

            update(OFF[i + 1] + B, OFF[i + 2], dots(y2, a1, True))
            y = [jnp.concatenate([u, v], axis=0) for u, v in zip(y, y2)]
            for j in range(i + 2, NB, 2):
                at = (j - i - 1) * B
                wide = min(2, NB - j) * B
                v = dots(part(y, slice(at, left)), part(a, slice(at, at + wide)), True)
                update(OFF[j], OFF[j + 1], v[:, :B])
                if wide > B:
                    update(OFF[j + 1], OFF[j + 2], v[B:, B:])
        for r, v in zip(y_refs, y):
            r[OFF[i] + B:OFF[i + 1]] = v
        zed = dots(split(b_ref[:, s:e]), ds, False)
        b_ref[:, e:] -= dots(split(zed), a, True)
        b_ref[:, s:e] = zed
        dinv = leaf(d)
    for j in range(NB - 1, 0, -1):
        x = split(b_ref[:, j * B:(j + 1) * B])
        y = [jnp.concatenate([r[OFF[i] + (j - i) * B:OFF[i] + (j - i + 1) * B] for i in range(j)], axis=1)
             for r in y_refs]
        b_ref[:, :j * B] -= dots(x, y, False)
    next(gather)
    hi, lo = split(b_ref[...] * jnp.broadcast_to(inv * (1.0 / jnp.sqrt(f32(K))), (1, K)), 2)
    o_ref[:, :K] = hi
    o_ref[:, K:] = lo
    for copy in k.started:
        copy.wait_send()


def solve(train_grads, queries, total):
    nq, n = queries.shape[0], train_grads.shape[0]
    return pl.pallas_call(
        functools.partial(kernel, total),
        out_shape=[jax.ShapeDtypeStruct((nq, 2 * K), bf), jax.ShapeDtypeStruct((2 * NX * n, K), f32)],
        in_specs=[pl.BlockSpec(memory_space=pl.ANY)] * 2,
        out_specs=[pl.BlockSpec(memory_space=pltpu.VMEM), pl.BlockSpec(memory_space=pl.ANY)],
        scratch_shapes=[
            pltpu.VMEM((n, K), f32),
            pltpu.VMEM((OFF[NB], B), f32), pltpu.VMEM((OFF[NB], B), f32), pltpu.VMEM((OFF[NB], B), f32),
            pltpu.VMEM((nq, K), f32)] + [pltpu.VMEM((OFF[NB], B), bf)] * 3 + [
            pltpu.SemaphoreType.DMA((NCOPY,)), pltpu.SemaphoreType.DMA((NCOPY,)), pltpu.SemaphoreType.DMA((3,))]
        + [s for c in CHUNKS for s in chunk_scratch(c)],
        compiler_params=pltpu.CompilerParams(
            collective_id=0, has_side_effects=True, vmem_limit_bytes=60 * 2**20),
    )(train_grads, queries)


def scores_kernel(g_ref, x_ref, o_ref):
    hi, lo = split(g_ref[...], 2)
    left = jnp.concatenate([hi, lo, hi], axis=1)
    right = jnp.concatenate([x_ref[:, :K], x_ref[:, :K], x_ref[:, K:]], axis=1)
    o_ref[...] = lax.dot_general(left, right, (((1,), (1,)), ((), ())), preferred_element_type=f32)


def scores_of(g, x):
    n, nq = g.shape[0], x.shape[0]
    step = 1024
    return pl.pallas_call(
        scores_kernel,
        grid=(n // step,),
        out_shape=jax.ShapeDtypeStruct((n, nq), f32),
        in_specs=[pl.BlockSpec((step, K), lambda i: (i, 0)), pl.BlockSpec((nq, 2 * K), lambda i: (0, 0))],
        out_specs=pl.BlockSpec((step, nq), lambda i: (i, 0)),
        compiler_params=pltpu.CompilerParams(vmem_limit_bytes=60 * 2**20),
    )(g, x)


def local(train_grads, queries):
    total = train_grads.shape[0] * lax.axis_size("train") * lax.axis_size("query")
    precond, block = solve(train_grads, queries, float(total))
    return scores_of(block, precond)


def solution(mesh):
    in_specs = (P(("train", "query"), None), P("query", None))
    out_specs = P("train", "query")
    return jax.shard_map(local, mesh=mesh, in_specs=in_specs, out_specs=out_specs, check_vma=False)
```

```python
import functools
import jax
import jax.numpy as jnp
from jax import lax
from jax.experimental import pallas as pl
from jax.experimental.pallas import tpu as pltpu
from jax.sharding import PartitionSpec as P

f32 = jnp.float32
bf = jnp.bfloat16
B = 128
NB = 8
K = B * NB
NY, NZ, NX = 4, 8, 4
MESH = pl.DeviceIdType.MESH
OFF = [sum((NB - i) * B for i in range(k)) for k in range(NB + 1)]
CHUNKS = [(0, 512, "y"), (512, 1024, "y"), (1536, 1024, "y"), (2560, 1024, "y"), (3584, 1024, "y")]
GATHER = -1
NCOPY = 7 * len(CHUNKS) + 12


def split(x, n=3):
    out = []
    for i in range(n):
        h = x.astype(bf)
        out.append(h)
        if i < n - 1:
            x = x - h.astype(f32)
    return out


TERMS = [(0, 0), (0, 1), (1, 0), (0, 2), (2, 0), (1, 1)]


def dots(a, b, nt):
    l = jnp.concatenate([a[i] for i, _ in TERMS], axis=1)
    r = jnp.concatenate([b[j] for _, j in TERMS], axis=1 if nt else 0)
    dims = (((1,), (1,) if nt else (0,)), ((), ()))
    return lax.dot_general(l, r, dims, preferred_element_type=f32)


def part(s, sl):
    return [x[sl] for x in s]


def leaf(a, G=16):
    nv=G//8; ng=B//G
    lane=lax.broadcasted_iota(jnp.int32,(8,B),1)
    sub=lax.broadcasted_iota(jnp.int32,(8,B),0)
    bl=lambda x,c: jnp.broadcast_to(x[:,c:c+1],(8,B))
    bs=lambda x,s: jnp.broadcast_to(x[s:s+1,:],(8,B))
    rows=[a[8*i:8*i+8,:] for i in range(16)]
    for g in range(ng):
        R=[rows[nv*g+v] for v in range(nv)]
        C=[[bl(R[v],G*g+c) for v in range(nv)] for c in range(G)]
        inb=(lane>=G*g)&(lane<G*g+G)
        RA=[jnp.where(inb, jnp.where(lane-G*g-8*v==sub,1.0,0.0), R[v]) for v in range(nv)]
        for j in range(0,G,2):
            jv,js=divmod(j,8)
            a0=bs(C[j][jv],js); b0=bs(C[j+1][jv],js); c0=bs(C[j+1][jv],js+1)
            r=pltpu.reciprocal(a0*c0-b0*b0,approx=True)
            u=[];w=[]
            for v in range(nv):
                cj,ck=C[j][v],C[j+1][v]
                if v==jv:
                    cj=jnp.where(sub==js,cj-1.0,cj); ck=jnp.where(sub==js+1,ck-1.0,ck)
                u.append(cj*c0-ck*b0); w.append(ck*a0-cj*b0)
            for c in range(j+2,G):
                x0=bs(C[c][jv],js); x1=bs(C[c][jv],js+1)
                for v in range(nv): C[c][v]=C[c][v]-(u[v]*x0+w[v]*x1)*r
            x0=bs(RA[jv],js); x1=bs(RA[jv],js+1)
            for v in range(nv): RA[v]=RA[v]-(u[v]*x0+w[v]*x1)*r
        new=list(rows)
        for v in range(nv): new[nv*g+v]=RA[v]
        near=[i for i in range(16) if i//nv==g+1]
        rb=[bs(RA[c//8],c%8) for c in range(G)] if near else []
        for i in near:
            p=[bl(rows[i],G*g+c)*rb[c] for c in range(G)]
            while len(p)>1: p=[p[2*k]+p[2*k+1] for k in range(len(p)//2)]
            new[i]=jnp.where(inb,0.0,rows[i])-p[0]
        rest=[i for i in range(16) if i//nv!=g and i not in near]
        zero=jnp.zeros((8,B),f32)
        d=lax.dot_general(jnp.concatenate([rows[i] for i in rest],0),
            jnp.concatenate([RA[i-nv*g] if i//nv==g else zero for i in range(16)],0),
            (((1,),(0,)),((),())),precision=lax.Precision.HIGHEST,preferred_element_type=f32)
        for m,i in enumerate(rest): new[i]=jnp.where(inb,0.0,rows[i])-d[8*m:8*m+8]
        rows=new
    return jnp.concatenate(rows,0)


class Links:
    def __init__(self, ssem, rsem):
        t, q = lax.axis_index("train"), lax.axis_index("query")
        self.y, self.z = t // NZ, lax.rem(t, NZ)
        self.x, self.c = q // 2, lax.rem(q, 2)
        self.ssem, self.rsem = ssem, rsem
        self.count = 0
        self.started = []

    def at(self, dx=0, dy=0, dz=0, dc=0):
        return (
            lax.rem(self.y + dy, NY) * NZ + lax.rem(self.z + dz, NZ),
            lax.rem(self.x + dx, NX) * 2 + lax.rem(self.c + dc, 2),
        )

    def send(self, src, dst, device):
        i = self.count
        self.count += 1
        copy = pltpu.make_async_remote_copy(
            src_ref=src, dst_ref=dst, send_sem=self.ssem.at[i], recv_sem=self.rsem.at[i],
            device_id=device, device_id_type=MESH)
        copy.start()
        self.started.append(copy)
        return copy


def arrive(copies):
    for copy in copies:
        copy.wait_recv()


class Exchange:
    def __init__(self, k, whole, copies):
        self.whole = whole
        i = k.count
        k.count += 1
        self.ssem, self.rsem = k.ssem.at[i], k.rsem.at[i]
        for src, dst, device in copies:
            pltpu.make_async_remote_copy(
                src_ref=src, dst_ref=dst, send_sem=self.ssem, recv_sem=self.rsem,
                device_id=device, device_id_type=MESH).start()

    def arrived(self):
        pltpu.make_async_copy(self.whole, self.whole, self.rsem).wait()

    def wait_send(self):
        pltpu.make_async_copy(self.whole, self.whole, self.ssem).wait()


def rows(base, i, size):
    return pl.ds(pl.multiple_of(base + i * size, 8), size)


def shares(chunk):
    n1, n2 = (NY, NZ) if chunk[2] == "y" else (NZ, NY)
    h = chunk[1] // 2
    return n1, n2, h, h // n1, h // n1 // n2


FAR_FIRST = {4: (2, 1, 3), 8: (4, 3, 5, 2, 6, 1, 7)}


def total_of(k, chunk, p_ref, o_ref, s1, w, s2, s3, sx):
    base = chunk[0]
    n1, n2, h, u, t = shares(chunk)
    c = k.c
    if chunk[2] == "y":
        i1, i2, to1, to2 = k.y, k.z, lambda d: k.at(dy=d), lambda d: k.at(dz=d)
    else:
        i1, i2, to1, to2 = k.z, k.y, lambda d: k.at(dz=d), lambda d: k.at(dy=d)
    sent = [Exchange(k, s1, [(p_ref.at[rows(base, 1 - c, h)], s1, k.at(dc=1))])]
    yield
    sent[0].arrived()
    w[...] = p_ref[rows(base, c, h)] + s1[...]
    some2, some_x = s2.at[pl.ds(0, n1 - 1)], sx.at[pl.ds(0, NX - 1)]
    sent.append(Exchange(k, some2, [
        (w.at[rows(0, lax.rem(i1 + d, n1), u)], s2.at[d - 1], to1(d)) for d in FAR_FIRST[n1]]))
    yield
    sent[1].arrived()
    v = w[rows(0, i1, u)]
    for d in range(n1 - 1):
        v = v + s2[d]
    s2[n1 - 1] = v
    sent.append(Exchange(k, s3, [
        (s2.at[n1 - 1, rows(0, lax.rem(i2 + d, n2), t)], s3.at[d - 1], to2(d)) for d in FAR_FIRST[n2]]))
    sent[0].wait_send()
    yield
    sent[2].arrived()
    v = s2[n1 - 1, rows(0, i2, t)]
    for d in range(n2 - 1):
        v = v + s3[d]
    sx[NX - 1] = v
    sent.append(Exchange(k, some_x, [(sx.at[NX - 1], sx.at[d - 1], k.at(dx=d)) for d in FAR_FIRST[NX]]))
    sent[1].wait_send()
    yield
    sent[3].arrived()
    own = pl.ds(pl.multiple_of(base + c * h + i1 * u + i2 * t, 8), t)
    o_ref[own] = (sx[0] + sx[1]) + (sx[2] + sx[3])
    sent.append(Exchange(k, s3, [(o_ref.at[own], o_ref.at[own], to2(d)) for d in FAR_FIRST[n2]]))
    sent[2].wait_send()
    yield
    sent[4].arrived()
    own = rows(base + c * h, i1, u)
    sent.append(Exchange(k, some2, [(o_ref.at[own], o_ref.at[own], to1(d)) for d in FAR_FIRST[n1]]))
    sent[3].wait_send()
    yield
    sent[5].arrived()
    own = rows(base, c, h)
    sent.append(Exchange(k, s1, [(o_ref.at[own], o_ref.at[own], k.at(dc=1))]))
    sent[4].wait_send()
    yield
    sent[6].arrived()
    k.started += sent[5:]
    yield


def chunk_scratch(chunk):
    n1, n2, h, u, t = shares(chunk)
    shapes = [(h, B), (h, B), (n1, u, B), (n2 - 1, t, B), (NX, t, B)]
    return [pltpu.VMEM(s, f32) for s in shapes]


def gathered(k, x_ref, g_ref, own_sem):
    n = x_ref.shape[0]
    half = n // 2
    mine = (k.x * 2 + k.c) * n
    below, above = (lax.rem(k.x + NX - 1, NX) * 2 + k.c) * n, (lax.rem(k.x + 1, NX) * 2 + k.c) * n
    across = (lax.rem(k.x + 2, NX) * 2 + k.c) * n
    at = lambda base, first, size: g_ref.at[pl.ds(pl.multiple_of(base + first, 8), size)]
    own = pltpu.make_async_copy(x_ref, at(mine, 0, n), own_sem)
    own.start()
    src = [x_ref.at[pl.ds(i * half, half)] for i in range(2)]
    up = [k.send(src[0], at(mine, 0, half), k.at(dx=1))]
    down = [k.send(src[1], at(mine, half, half), k.at(dx=NX - 1))]
    yield
    up.append(k.send(src[1], at(mine, half, half), k.at(dx=1)))
    down.append(k.send(src[0], at(mine, 0, half), k.at(dx=NX - 1)))
    core = [k.send(x_ref, at(mine, 0, n), k.at(dc=1))]
    arrive([up[0], down[0]])
    lo, hi = at(below, 0, half), at(above, half, half)
    far = [k.send(lo, lo, k.at(dx=1)), k.send(hi, hi, k.at(dx=NX - 1))]
    yield
    arrive([up[1], down[1]])
    for base in (below, above):
        block = at(base, 0, n)
        core.append(k.send(block, block, k.at(dc=1)))
    yield
    arrive(far)
    block = at(across, 0, n)
    core.append(k.send(block, block, k.at(dc=1)))
    yield
    own.wait()
    arrive(core)
    yield


def kernel(total, x_hbm, q_hbm, o_ref, g_ref, x_ref, p_ref, f_ref, m_ref, b_ref, y0_ref, y1_ref, y2_ref,
           ssem, rsem, lsem, *scratch):
    y_refs = (y0_ref, y1_ref, y2_ref)
    k = Links(ssem, rsem)
    load = pltpu.make_async_copy(x_hbm, x_ref, lsem.at[0])
    load.start()
    q_load = pltpu.make_async_copy(q_hbm, b_ref, lsem.at[2])
    q_load.start()
    peers = [k.at(dc=1)] + [k.at(dx=d) for d in range(1, NX)]
    peers += [k.at(dy=d) for d in range(1, NY)] + [k.at(dz=d) for d in range(1, NZ)]
    barrier = pltpu.get_barrier_semaphore()
    for device in peers:
        pl.semaphore_signal(barrier, inc=1, device_id=device, device_id_type=MESH)
    load.wait()

    def gram(j):
        v = lax.dot_general(
            x_ref[:, j * B:], x_ref[:, j * B:(j + 1) * B], (((0,), (0,)), ((), ())),
            precision=lax.Precision.HIGHEST, preferred_element_type=f32)
        if j == 0:
            p_ref[:3 * B], p_ref[4 * B:9 * B] = v[:3 * B], v[3 * B:]
        elif j == 1:
            p_ref[3 * B:4 * B], p_ref[9 * B:15 * B] = v[:B], v[B:]
        else:
            p_ref[OFF[j]:OFF[j + 1]] = v

    def top(j):
        return f_ref[3 * B:4 * B] if j == 1 else f_ref[OFF[j]:OFF[j] + B]

    def below(j):
        return f_ref[OFF[j] + B:OFF[j + 1]]

    row_at = lax.broadcasted_iota(jnp.int32, (B, B), 0)
    column_at = lax.broadcasted_iota(jnp.int32, (B, B), 1)
    corner = (row_at == 0) & (column_at == B - 1)
    eye = row_at == column_at
    squares = jnp.sum(x_ref[...] * x_ref[...], axis=0, keepdims=True) * (1.0 / total)
    gram(0)
    gram(1)
    p_ref[:B] = jnp.where(corner, jnp.sum(squares, axis=1, keepdims=True), p_ref[:B])
    pl.semaphore_wait(barrier, len(peers))
    sums = [total_of(k, c, p_ref, f_ref, *scratch[5 * i:5 * i + 5]) for i, c in enumerate(CHUNKS)]
    gather = gathered(k, x_hbm, g_ref, lsem.at[1])
    done = [0] * len(sums)

    def go(*chunks):
        for i in chunks:
            next(sums[i])
            done[i] += 1

    go(0)
    next(gather)
    gram(2)
    go(1, 0)
    for j in range(3, NB):
        gram(j)
    go(2, 3, 4, 1, 2, 3, 4)
    go(0, 1, 0, 2, 0, 1, 4, 3, 1, 0, 2, 3, 2, 0, 4, 3)
    next(gather)
    go(1, 0)
    d = f_ref[:B]
    trace = d[0:1, B - 1:B]
    damp = 0.1 * trace / K
    inv = 1.0 / damp
    scale = jnp.broadcast_to(inv * (1.0 / total), (1, B))
    d = jnp.where(corner, d[B - 1:B, 0:1], d) * scale
    dinv = leaf(jnp.where(eye, d + 1.0, d))
    q_load.wait()
    at_start = {0: (2, 4), 1: (2, 4), 2: (3,), 4: (4, GATHER), 6: (GATHER,)}
    at_next = {0: (1,), 1: (2,)}
    at_leaf = {0: (3,), 1: (3,), 3: (4,)}

    def advance(due):
        for j in due:
            if j == GATHER:
                next(gather)
            else:
                go(j)

    for i in range(NB):
        s, e = i * B, i * B + B
        left = (NB - 1 - i) * B
        ds = split(dinv)
        if i == NB - 1:
            b_ref[:, s:e] = dots(split(b_ref[:, s:e]), ds, False)
            break
        advance(at_start.get(i, ()))
        if i == 0:
            a1 = split(f_ref[B:2 * B] * scale)
            y = split(dots(a1, ds, False))
            d = top(1) * scale - dots(y, a1, True)
            advance(at_leaf[0])
            dinv = leaf(jnp.where(eye, d + 1.0, d))
            advance((1,))
            zed = dots(split(b_ref[:, s:e]), ds, False)
            advance(at_next[0])
            a2 = split(jnp.concatenate([f_ref[2 * B:3 * B], f_ref[4 * B:9 * B]], axis=0) * scale)
        else:
            zed = dots(split(b_ref[:, s:e]), ds, False)
            advance(at_next.get(i, ()))
            a = split(below(i) * scale + m_ref[OFF[i] + B:OFF[i + 1]])
            a1, a2 = part(a, slice(0, B)), part(a, slice(B, left))
            y = split(dots(a1, ds, False))
            v = dots(y, a1, True)
            d = top(i + 1) * scale + (m_ref[OFF[i + 1]:OFF[i + 1] + B] - v)
            d = jnp.where(eye, d + 1.0, d)
        if i < NB - 2:
            y2 = split(dots(a2, ds, False))

            def update(lo, hi, v):
                m_ref[lo:hi] = -v if i == 0 else m_ref[lo:hi] - v

            update(OFF[i + 1] + B, OFF[i + 2], dots(y2, a1, True))
            a = [jnp.concatenate([u, v], axis=0) for u, v in zip(a1, a2)]
            y = [jnp.concatenate([u, v], axis=0) for u, v in zip(y, y2)]
            for j in range(i + 2, NB, 2):
                at = (j - i - 1) * B
                wide = min(2, NB - j) * B
                v = dots(part(y, slice(at, left)), part(a, slice(at, at + wide)), True)
                update(OFF[j], OFF[j + 1], v[:, :B])
                if wide > B:
                    update(OFF[j + 1], OFF[j + 2], v[B:, B:])
        for r, v in zip(y_refs, y):
            r[OFF[i] + B:OFF[i + 1]] = v
        b_ref[:, e:] -= dots(split(zed), a, True)
        b_ref[:, s:e] = zed
        if i > 0:
            advance(at_leaf.get(i, ()))
            dinv = leaf(d)
    for j in range(NB - 1, 0, -1):
        x = split(b_ref[:, j * B:(j + 1) * B])
        y = [[r[OFF[i] + (j - i) * B:OFF[i] + (j - i + 1) * B] for r in y_refs] for i in range(j)]
        b_ref[:, (j - 1) * B:j * B] -= dots(x, y[j - 1], False)
        if j > 1:
            y = [jnp.concatenate([y[i][m] for i in range(j - 1)], axis=1) for m in range(3)]
            b_ref[:, :(j - 1) * B] -= dots(x, y, False)
    next(gather)
    hi, lo = split(b_ref[...] * jnp.broadcast_to(inv * (1.0 / jnp.sqrt(f32(K))), (1, K)), 2)
    o_ref[:, :K] = hi
    o_ref[:, K:] = lo
    for copy in k.started:
        copy.wait_send()


def solve(train_grads, queries, total):
    nq, n = queries.shape[0], train_grads.shape[0]
    return pl.pallas_call(
        functools.partial(kernel, total),
        out_shape=[jax.ShapeDtypeStruct((nq, 2 * K), bf), jax.ShapeDtypeStruct((2 * NX * n, K), f32)],
        in_specs=[pl.BlockSpec(memory_space=pl.ANY)] * 2,
        out_specs=[pl.BlockSpec(memory_space=pltpu.VMEM), pl.BlockSpec(memory_space=pl.ANY)],
        scratch_shapes=[
            pltpu.VMEM((n, K), f32),
            pltpu.VMEM((OFF[NB], B), f32), pltpu.VMEM((OFF[NB], B), f32), pltpu.VMEM((OFF[NB], B), f32),
            pltpu.VMEM((nq, K), f32)] + [pltpu.VMEM((OFF[NB], B), bf)] * 3 + [
            pltpu.SemaphoreType.DMA((NCOPY,)), pltpu.SemaphoreType.DMA((NCOPY,)), pltpu.SemaphoreType.DMA((3,))]
        + [s for c in CHUNKS for s in chunk_scratch(c)],
        compiler_params=pltpu.CompilerParams(
            collective_id=0, has_side_effects=True, vmem_limit_bytes=60 * 2**20),
    )(train_grads, queries)


def scores_kernel(g_ref, x_ref, o_ref):
    hi, lo = split(g_ref[...], 2)
    left = jnp.concatenate([hi, lo, hi], axis=1)
    right = jnp.concatenate([x_ref[:, :K], x_ref[:, :K], x_ref[:, K:]], axis=1)
    o_ref[...] = lax.dot_general(left, right, (((1,), (1,)), ((), ())), preferred_element_type=f32)


def scores_of(g, x):
    n, nq = g.shape[0], x.shape[0]
    step = 1024
    return pl.pallas_call(
        scores_kernel,
        grid=(n // step,),
        out_shape=jax.ShapeDtypeStruct((n, nq), f32),
        in_specs=[pl.BlockSpec((step, K), lambda i: (i, 0)), pl.BlockSpec((nq, 2 * K), lambda i: (0, 0))],
        out_specs=pl.BlockSpec((step, nq), lambda i: (i, 0)),
        compiler_params=pltpu.CompilerParams(vmem_limit_bytes=60 * 2**20),
    )(g, x)


def local(train_grads, queries):
    total = train_grads.shape[0] * lax.axis_size("train") * lax.axis_size("query")
    precond, block = solve(train_grads, queries, float(total))
    return scores_of(block, precond)


def solution(mesh):
    in_specs = (P(("train", "query"), None), P("query", None))
    out_specs = P("train", "query")
    return jax.shard_map(local, mesh=mesh, in_specs=in_specs, out_specs=out_specs, check_vma=False)
```

```python
import functools
import jax
import jax.numpy as jnp
from jax import lax
from jax.experimental import pallas as pl
from jax.experimental.pallas import tpu as pltpu
from jax.sharding import PartitionSpec as P

f32 = jnp.float32
bf = jnp.bfloat16
B = 128
NB = 8
K = B * NB
NY, NZ, NX = 4, 8, 4
MESH = pl.DeviceIdType.MESH
OFF = [sum((NB - i) * B for i in range(k)) for k in range(NB + 1)]
CHUNKS = [(0, 512, "y"), (512, 1024, "y"), (1536, 1024, "y"), (2560, 1024, "y"), (3584, 1024, "y")]
GATHER = -1
NCOPY = 7 * len(CHUNKS) + 12


def split(x, n=3):
    out = []
    for i in range(n):
        h = x.astype(bf)
        out.append(h)
        if i < n - 1:
            x = x - h.astype(f32)
    return out


TERMS = [(0, 0), (0, 1), (1, 0), (0, 2), (2, 0), (1, 1)]


def dots(a, b, nt):
    l = jnp.concatenate([a[i] for i, _ in TERMS], axis=1)
    r = jnp.concatenate([b[j] for _, j in TERMS], axis=1 if nt else 0)
    dims = (((1,), (1,) if nt else (0,)), ((), ()))
    return lax.dot_general(l, r, dims, preferred_element_type=f32)


def part(s, sl):
    return [x[sl] for x in s]


def leaf(a, G=16):
    nv=G//8; ng=B//G
    lane=lax.broadcasted_iota(jnp.int32,(8,B),1)
    sub=lax.broadcasted_iota(jnp.int32,(8,B),0)
    bl=lambda x,c: jnp.broadcast_to(x[:,c:c+1],(8,B))
    bs=lambda x,s: jnp.broadcast_to(x[s:s+1,:],(8,B))
    rows=[a[8*i:8*i+8,:] for i in range(16)]
    for g in range(ng):
        R=[rows[nv*g+v] for v in range(nv)]
        C=[[bl(R[v],G*g+c) for v in range(nv)] for c in range(G)]
        inb=(lane>=G*g)&(lane<G*g+G)
        RA=[jnp.where(inb, jnp.where(lane-G*g-8*v==sub,1.0,0.0), R[v]) for v in range(nv)]
        for j in range(0,G,2):
            jv,js=divmod(j,8)
            a0=bs(C[j][jv],js); b0=bs(C[j+1][jv],js); c0=bs(C[j+1][jv],js+1)
            r=pltpu.reciprocal(a0*c0-b0*b0,approx=True)
            u=[];w=[]
            for v in range(nv):
                cj,ck=C[j][v],C[j+1][v]
                if v==jv:
                    cj=jnp.where(sub==js,cj-1.0,cj); ck=jnp.where(sub==js+1,ck-1.0,ck)
                u.append(cj*c0-ck*b0); w.append(ck*a0-cj*b0)
            for c in range(j+2,G):
                x0=bs(C[c][jv],js); x1=bs(C[c][jv],js+1)
                for v in range(nv): C[c][v]=C[c][v]-(u[v]*x0+w[v]*x1)*r
            x0=bs(RA[jv],js); x1=bs(RA[jv],js+1)
            for v in range(nv): RA[v]=RA[v]-(u[v]*x0+w[v]*x1)*r
        new=list(rows)
        for v in range(nv): new[nv*g+v]=RA[v]
        near=[i for i in range(16) if i//nv==g+1]
        rb=[bs(RA[c//8],c%8) for c in range(G)] if near else []
        for i in near:
            p=[bl(rows[i],G*g+c)*rb[c] for c in range(G)]
            while len(p)>1: p=[p[2*k]+p[2*k+1] for k in range(len(p)//2)]
            new[i]=jnp.where(inb,0.0,rows[i])-p[0]
        rest=[i for i in range(16) if i//nv!=g and i not in near]
        zero=jnp.zeros((8,B),f32)
        d=lax.dot_general(jnp.concatenate([rows[i] for i in rest],0),
            jnp.concatenate([RA[i-nv*g] if i//nv==g else zero for i in range(16)],0),
            (((1,),(0,)),((),())),precision=lax.Precision.HIGHEST,preferred_element_type=f32)
        for m,i in enumerate(rest): new[i]=jnp.where(inb,0.0,rows[i])-d[8*m:8*m+8]
        rows=new
    return jnp.concatenate(rows,0)


class Links:
    def __init__(self, ssem, rsem):
        t, q = lax.axis_index("train"), lax.axis_index("query")
        self.y, self.z = t // NZ, lax.rem(t, NZ)
        self.x, self.c = q // 2, lax.rem(q, 2)
        self.ssem, self.rsem = ssem, rsem
        self.count = 0
        self.started = []

    def at(self, dx=0, dy=0, dz=0, dc=0):
        return (
            lax.rem(self.y + dy, NY) * NZ + lax.rem(self.z + dz, NZ),
            lax.rem(self.x + dx, NX) * 2 + lax.rem(self.c + dc, 2),
        )

    def send(self, src, dst, device):
        i = self.count
        self.count += 1
        copy = pltpu.make_async_remote_copy(
            src_ref=src, dst_ref=dst, send_sem=self.ssem.at[i], recv_sem=self.rsem.at[i],
            device_id=device, device_id_type=MESH)
        copy.start()
        self.started.append(copy)
        return copy


def arrive(copies):
    for copy in copies:
        copy.wait_recv()


class Exchange:
    def __init__(self, k, whole, copies):
        self.whole = whole
        i = k.count
        k.count += 1
        self.ssem, self.rsem = k.ssem.at[i], k.rsem.at[i]
        for src, dst, device in copies:
            pltpu.make_async_remote_copy(
                src_ref=src, dst_ref=dst, send_sem=self.ssem, recv_sem=self.rsem,
                device_id=device, device_id_type=MESH).start()

    def arrived(self):
        pltpu.make_async_copy(self.whole, self.whole, self.rsem).wait()

    def wait_send(self):
        pltpu.make_async_copy(self.whole, self.whole, self.ssem).wait()


def rows(base, i, size):
    return pl.ds(pl.multiple_of(base + i * size, 8), size)


def shares(chunk):
    n1, n2 = (NY, NZ) if chunk[2] == "y" else (NZ, NY)
    h = chunk[1] // 2
    return n1, n2, h, h // n1, h // n1 // n2


FAR_FIRST = {4: (2, 1, 3), 8: (4, 3, 5, 2, 6, 1, 7)}


def total_of(k, chunk, p_ref, o_ref, s1, w, s2, s3, sx):
    base = chunk[0]
    n1, n2, h, u, t = shares(chunk)
    c = k.c
    if chunk[2] == "y":
        i1, i2, to1, to2 = k.y, k.z, lambda d: k.at(dy=d), lambda d: k.at(dz=d)
    else:
        i1, i2, to1, to2 = k.z, k.y, lambda d: k.at(dz=d), lambda d: k.at(dy=d)
    sent = [Exchange(k, s1, [(p_ref.at[rows(base, 1 - c, h)], s1, k.at(dc=1))])]
    yield
    sent[0].arrived()
    w[...] = p_ref[rows(base, c, h)] + s1[...]
    some2, some_x = s2.at[pl.ds(0, n1 - 1)], sx.at[pl.ds(0, NX - 1)]
    sent.append(Exchange(k, some2, [
        (w.at[rows(0, lax.rem(i1 + d, n1), u)], s2.at[d - 1], to1(d)) for d in FAR_FIRST[n1]]))
    yield
    sent[1].arrived()
    v = w[rows(0, i1, u)]
    for d in range(n1 - 1):
        v = v + s2[d]
    s2[n1 - 1] = v
    sent.append(Exchange(k, s3, [
        (s2.at[n1 - 1, rows(0, lax.rem(i2 + d, n2), t)], s3.at[d - 1], to2(d)) for d in FAR_FIRST[n2]]))
    sent[0].wait_send()
    yield
    sent[2].arrived()
    v = s2[n1 - 1, rows(0, i2, t)]
    for d in range(n2 - 1):
        v = v + s3[d]
    sx[NX - 1] = v
    sent.append(Exchange(k, some_x, [(sx.at[NX - 1], sx.at[d - 1], k.at(dx=d)) for d in FAR_FIRST[NX]]))
    sent[1].wait_send()
    yield
    sent[3].arrived()
    own = pl.ds(pl.multiple_of(base + c * h + i1 * u + i2 * t, 8), t)
    o_ref[own] = (sx[0] + sx[1]) + (sx[2] + sx[3])
    sent.append(Exchange(k, s3, [(o_ref.at[own], o_ref.at[own], to2(d)) for d in FAR_FIRST[n2]]))
    sent[2].wait_send()
    yield
    sent[4].arrived()
    own = rows(base + c * h, i1, u)
    sent.append(Exchange(k, some2, [(o_ref.at[own], o_ref.at[own], to1(d)) for d in FAR_FIRST[n1]]))
    sent[3].wait_send()
    yield
    sent[5].arrived()
    own = rows(base, c, h)
    sent.append(Exchange(k, s1, [(o_ref.at[own], o_ref.at[own], k.at(dc=1))]))
    sent[4].wait_send()
    yield
    sent[6].arrived()
    k.started += sent[5:]
    yield


def chunk_scratch(chunk):
    n1, n2, h, u, t = shares(chunk)
    shapes = [(h, B), (h, B), (n1, u, B), (n2 - 1, t, B), (NX, t, B)]
    return [pltpu.VMEM(s, f32) for s in shapes]


def gathered(k, x_ref, g_ref, own_sem):
    n = x_ref.shape[0]
    half = n // 2
    mine = (k.x * 2 + k.c) * n
    below, above = (lax.rem(k.x + NX - 1, NX) * 2 + k.c) * n, (lax.rem(k.x + 1, NX) * 2 + k.c) * n
    across = (lax.rem(k.x + 2, NX) * 2 + k.c) * n
    at = lambda base, first, size: g_ref.at[pl.ds(pl.multiple_of(base + first, 8), size)]
    own = pltpu.make_async_copy(x_ref, at(mine, 0, n), own_sem)
    own.start()
    src = [x_ref.at[pl.ds(i * half, half)] for i in range(2)]
    up = [k.send(src[0], at(mine, 0, half), k.at(dx=1))]
    down = [k.send(src[1], at(mine, half, half), k.at(dx=NX - 1))]
    yield
    up.append(k.send(src[1], at(mine, half, half), k.at(dx=1)))
    down.append(k.send(src[0], at(mine, 0, half), k.at(dx=NX - 1)))
    core = [k.send(x_ref, at(mine, 0, n), k.at(dc=1))]
    arrive([up[0], down[0]])
    lo, hi = at(below, 0, half), at(above, half, half)
    far = [k.send(lo, lo, k.at(dx=1)), k.send(hi, hi, k.at(dx=NX - 1))]
    yield
    arrive([up[1], down[1]])
    for base in (below, above):
        block = at(base, 0, n)
        core.append(k.send(block, block, k.at(dc=1)))
    yield
    arrive(far)
    block = at(across, 0, n)
    core.append(k.send(block, block, k.at(dc=1)))
    yield
    own.wait()
    arrive(core)
    yield


def kernel(total, x_hbm, q_hbm, o_ref, g_ref, x_ref, p_ref, f_ref, m_ref, b_ref, y0_ref, y1_ref, y2_ref,
           ssem, rsem, lsem, *scratch):
    y_refs = (y0_ref, y1_ref, y2_ref)
    k = Links(ssem, rsem)
    load = pltpu.make_async_copy(x_hbm, x_ref, lsem.at[0])
    load.start()
    q_load = pltpu.make_async_copy(q_hbm, b_ref, lsem.at[2])
    q_load.start()
    peers = [k.at(dc=1)] + [k.at(dx=d) for d in range(1, NX)]
    peers += [k.at(dy=d) for d in range(1, NY)] + [k.at(dz=d) for d in range(1, NZ)]
    barrier = pltpu.get_barrier_semaphore()
    for device in peers:
        pl.semaphore_signal(barrier, inc=1, device_id=device, device_id_type=MESH)
    load.wait()

    def gram(j):
        v = lax.dot_general(
            x_ref[:, j * B:], x_ref[:, j * B:(j + 1) * B], (((0,), (0,)), ((), ())),
            precision=lax.Precision.HIGHEST, preferred_element_type=f32)
        if j == 0:
            p_ref[:3 * B], p_ref[4 * B:9 * B] = v[:3 * B], v[3 * B:]
        elif j == 1:
            p_ref[3 * B:4 * B], p_ref[9 * B:15 * B] = v[:B], v[B:]
        else:
            p_ref[OFF[j]:OFF[j + 1]] = v

    def top(j):
        return f_ref[3 * B:4 * B] if j == 1 else f_ref[OFF[j]:OFF[j] + B]

    def below(j):
        return f_ref[OFF[j] + B:OFF[j + 1]]

    row_at = lax.broadcasted_iota(jnp.int32, (B, B), 0)
    column_at = lax.broadcasted_iota(jnp.int32, (B, B), 1)
    corner = (row_at == 0) & (column_at == B - 1)
    eye = row_at == column_at
    squares = jnp.sum(x_ref[...] * x_ref[...], axis=0, keepdims=True) * (1.0 / total)
    gram(0)
    gram(1)
    p_ref[:B] = jnp.where(corner, jnp.sum(squares, axis=1, keepdims=True), p_ref[:B])
    pl.semaphore_wait(barrier, len(peers))
    sums = [total_of(k, c, p_ref, f_ref, *scratch[5 * i:5 * i + 5]) for i, c in enumerate(CHUNKS)]
    gather = gathered(k, x_hbm, g_ref, lsem.at[1])
    done = [0] * len(sums)

    def go(*chunks):
        for i in chunks:
            next(sums[i])
            done[i] += 1

    go(0)
    next(gather)
    gram(2)
    go(1, 0)
    for j in range(3, NB):
        gram(j)
    go(2, 3, 4, 1, 2, 3, 4)
    go(0, 1, 0, 2, 0, 1, 4, 3, 1, 0, 2, 3, 2, 0, 4, 3)
    next(gather)
    go(1, 0)
    d = f_ref[:B]
    trace = d[0:1, B - 1:B]
    damp = 0.1 * trace / K
    inv = 1.0 / damp
    scale = jnp.broadcast_to(inv * (1.0 / total), (1, B))
    d = jnp.where(corner, d[B - 1:B, 0:1], d) * scale
    dinv = leaf(jnp.where(eye, d + 1.0, d))
    q_load.wait()
    at_start = {0: (2,), 1: (2,), 2: (3, 4), 4: (4, GATHER), 6: (GATHER,)}
    at_next = {0: (1,), 1: (2,), 2: (3,)}
    at_leaf = {0: (1,), 3: (4,)}

    def advance(due):
        for j in due:
            if j == GATHER:
                next(gather)
            else:
                go(j)

    for i in range(NB):
        s, e = i * B, i * B + B
        left = (NB - 1 - i) * B
        ds = split(dinv)
        if i == NB - 1:
            b_ref[:, s:e] = dots(split(b_ref[:, s:e]), ds, False)
            break
        advance(at_start.get(i, ()))
        if i == 0:
            a1 = split(f_ref[B:2 * B] * scale)
            y = split(dots(a1, ds, False))
            d = top(1) * scale - dots(y, a1, True)
            advance(at_leaf[0])
            dinv = leaf(jnp.where(eye, d + 1.0, d))
            advance((3, 4))
            zed = dots(split(b_ref[:, s:e]), ds, False)
            advance(at_next[0])
            a2 = split(jnp.concatenate([f_ref[2 * B:3 * B], f_ref[4 * B:9 * B]], axis=0) * scale)
        else:
            zed = dots(split(b_ref[:, s:e]), ds, False)
            advance(at_next.get(i, ()))
            a = split(below(i) * scale + m_ref[OFF[i] + B:OFF[i + 1]])
            a1, a2 = part(a, slice(0, B)), part(a, slice(B, left))
            y = split(dots(a1, ds, False))
            v = dots(y, a1, True)
            d = top(i + 1) * scale + (m_ref[OFF[i + 1]:OFF[i + 1] + B] - v)
            d = jnp.where(eye, d + 1.0, d)
        if i < NB - 2:
            y2 = split(dots(a2, ds, False))

            def update(lo, hi, v):
                m_ref[lo:hi] = -v if i == 0 else m_ref[lo:hi] - v

            update(OFF[i + 1] + B, OFF[i + 2], dots(y2, a1, True))
            a = [jnp.concatenate([u, v], axis=0) for u, v in zip(a1, a2)]
            y = [jnp.concatenate([u, v], axis=0) for u, v in zip(y, y2)]
            for j in range(i + 2, NB, 2):
                at = (j - i - 1) * B
                wide = min(2, NB - j) * B
                v = dots(part(y, slice(at, left)), part(a, slice(at, at + wide)), True)
                update(OFF[j], OFF[j + 1], v[:, :B])
                if wide > B:
                    update(OFF[j + 1], OFF[j + 2], v[B:, B:])
        for r, v in zip(y_refs, y):
            r[OFF[i] + B:OFF[i + 1]] = v
        b_ref[:, e:] -= dots(split(zed), a, True)
        b_ref[:, s:e] = zed
        if i > 0:
            advance(at_leaf.get(i, ()))
            dinv = leaf(d)
    for j in range(NB - 1, 0, -1):
        x = split(b_ref[:, j * B:(j + 1) * B])
        y = [[r[OFF[i] + (j - i) * B:OFF[i] + (j - i + 1) * B] for r in y_refs] for i in range(j)]
        b_ref[:, (j - 1) * B:j * B] -= dots(x, y[j - 1], False)
        if j > 1:
            y = [jnp.concatenate([y[i][m] for i in range(j - 1)], axis=1) for m in range(3)]
            b_ref[:, :(j - 1) * B] -= dots(x, y, False)
    next(gather)
    hi, lo = split(b_ref[...] * jnp.broadcast_to(inv * (1.0 / jnp.sqrt(f32(K))), (1, K)), 2)
    o_ref[:, :K] = hi
    o_ref[:, K:] = lo
    for copy in k.started:
        copy.wait_send()


def solve(train_grads, queries, total):
    nq, n = queries.shape[0], train_grads.shape[0]
    return pl.pallas_call(
        functools.partial(kernel, total),
        out_shape=[jax.ShapeDtypeStruct((nq, 2 * K), bf), jax.ShapeDtypeStruct((2 * NX * n, K), f32)],
        in_specs=[pl.BlockSpec(memory_space=pl.ANY)] * 2,
        out_specs=[pl.BlockSpec(memory_space=pltpu.VMEM), pl.BlockSpec(memory_space=pl.ANY)],
        scratch_shapes=[
            pltpu.VMEM((n, K), f32),
            pltpu.VMEM((OFF[NB], B), f32), pltpu.VMEM((OFF[NB], B), f32), pltpu.VMEM((OFF[NB], B), f32),
            pltpu.VMEM((nq, K), f32)] + [pltpu.VMEM((OFF[NB], B), bf)] * 3 + [
            pltpu.SemaphoreType.DMA((NCOPY,)), pltpu.SemaphoreType.DMA((NCOPY,)), pltpu.SemaphoreType.DMA((3,))]
        + [s for c in CHUNKS for s in chunk_scratch(c)],
        compiler_params=pltpu.CompilerParams(
            collective_id=0, has_side_effects=True, vmem_limit_bytes=60 * 2**20),
    )(train_grads, queries)


def scores_kernel(g_ref, x_ref, o_ref):
    hi, lo = split(g_ref[...], 2)
    left = jnp.concatenate([hi, lo, hi], axis=1)
    right = jnp.concatenate([x_ref[:, :K], x_ref[:, :K], x_ref[:, K:]], axis=1)
    o_ref[...] = lax.dot_general(left, right, (((1,), (1,)), ((), ())), preferred_element_type=f32)


def scores_of(g, x):
    n, nq = g.shape[0], x.shape[0]
    step = 1024
    return pl.pallas_call(
        scores_kernel,
        grid=(n // step,),
        out_shape=jax.ShapeDtypeStruct((n, nq), f32),
        in_specs=[pl.BlockSpec((step, K), lambda i: (i, 0)), pl.BlockSpec((nq, 2 * K), lambda i: (0, 0))],
        out_specs=pl.BlockSpec((step, nq), lambda i: (i, 0)),
        compiler_params=pltpu.CompilerParams(vmem_limit_bytes=60 * 2**20),
    )(g, x)


def local(train_grads, queries):
    total = train_grads.shape[0] * lax.axis_size("train") * lax.axis_size("query")
    precond, block = solve(train_grads, queries, float(total))
    return scores_of(block, precond)


def solution(mesh):
    in_specs = (P(("train", "query"), None), P("query", None))
    out_specs = P("train", "query")
    return jax.shard_map(local, mesh=mesh, in_specs=in_specs, out_specs=out_specs, check_vma=False)
```
